32 devices in a mesh: dp: 1, dap: 32 (over z, y, x, core).
Axes of the slice: x: 2, y: 2, z: 4, core: 2. Of those that a mesh axis runs over, the one named last changes fastest.
Arguments:
- alignment: bfloat16 [128, 256, 256], P(('dp', 'dap')), may hold values from -6 to 6
- pair_rep: bfloat16 [256, 256, 128], P(('dp', 'dap')), may hold values from -6 to 6
- align_mask: int32 [128, 256], P(('dp', 'dap')), may hold values 0 or 1
- residue_mask: int32 [256], P('dp'), may hold values 0 or 1
- row_gain: float32 [256], replicated, may hold values from 0.1 to 1.9
- pair_gain: float32 [128], replicated, may hold values from 0.1 to 1.9
- row_bias: bfloat16 [128, 8], replicated, may hold values from -0.5 to 0.5
- row_scoring: bfloat16 [256, 512], replicated, may hold values from -4 to 4
- row_values: bfloat16 [256, 512], replicated, may hold values from -0.375 to 0.375
- row_output: bfloat16 [256, 256], replicated, may hold values from -0.375 to 0.375
- column_gain: float32 [256], replicated, may hold values from 0.1 to 1.9
- column_scoring: bfloat16 [256, 512], replicated, may hold values from -4 to 4
- column_values: bfloat16 [256, 512], replicated, may hold values from -0.375 to 0.375
- column_output: bfloat16 [256, 256], replicated, may hold values from -0.375 to 0.375
- outer_gain: float32 [256], replicated, may hold values from 0.1 to 1.9
- outer_inputs: bfloat16 [256, 64], replicated, may hold values from -0.375 to 0.375
- outer_output: bfloat16 [1024, 128], replicated, may hold values from -1 to 1
Outputs:
- new_alignment: bfloat16 [128, 256, 256], P(('dp', 'dap'))
- new_pair: bfloat16 [256, 256, 128], P(('dp', 'dap'))
The draws below stay inside these ranges and needn't reach their ends.
All inputs are finite; a program needn't handle non-finite values. No bound on the sum of `align_mask` on one device may be relied on, other than what follows from the above.
Results may differ from the reference program's by a relative error of at most 0.012.
The reference program's roundings to bfloat16 on the way count: a program that leaves them out, or rounds other values in their place, can miss the bound.
Values may be sent and summed in bfloat16 or wider, within the bound.
A program may use at most 64 MiB of HBM per device.

```python
import math
import jax
import jax.numpy as jnp
from jax import lax

C_M = 256
C_Z = 128
HEADS = 8
HEAD = 32
C_OPM = 32
N_SEQ = 128
N_RES = 256


def query_key(key):
    base = jax.random.normal(jax.random.fold_in(key, 11), (C_M, C_M), jnp.float32)
    other = jax.random.normal(jax.random.fold_in(key, 14), (C_M, C_M), jnp.float32)
    query_part = base * C_M ** (-0.5)
    key_part = other * C_M ** (-0.5)
    joined = jnp.clip(jnp.concatenate([query_part, key_part], axis=1), -4.0, 4.0)
    return joined.astype(jnp.bfloat16)


def draw_row_scoring(key, part):
    return query_key(jax.random.fold_in(key, 1))


def draw_column_scoring(key, part):
    return query_key(jax.random.fold_in(key, 2))


def with_ends(array, own_key, low, largest):
    longest = array.shape.index(max(array.shape))
    spots = []
    for shift in (0, 1):
        where = [jax.random.randint(jax.random.fold_in(own_key, axis), (), 0, length) for axis, length in enumerate(array.shape)]
        where[longest] = (where[longest] + shift) % array.shape[longest]
        spots.append(tuple(where))
    return array.at[spots[0]].set(low).at[spots[1]].set(largest)


def steps_of(rng, dims, cuts, smallest, largest):
    def one(dim, blocks):
        steps = jax.random.uniform(jax.random.fold_in(jax.random.fold_in(rng, 6), dim), (blocks,), jnp.float32, smallest / len(cuts), largest / len(cuts))
        return jnp.repeat(jnp.exp(steps), dims[dim] // blocks).reshape((-1,) + (1,) * (len(dims) - dim - 1))

    level = one(*cuts[0])
    for cut in cuts[1:]:
        level = level * one(*cut)
    return level


def scatter_about(stream_key, extent, deviation, bound, cuts=(), kind=jnp.bfloat16):
    result = jax.random.normal(stream_key, extent, jnp.float32) * deviation
    if len(cuts) > 0:
        result = steps_of(stream_key, extent, cuts, -0.22, 0.18) * result
    return jnp.clip(result, min=-bound, max=bound).astype(kind)


def setup_inputs(seed: int = 0, part: int = 0) -> dict:
    arg_keys = jax.random.split(jax.random.key(seed), 18)
    part_keys = jax.random.split(jax.random.fold_in(arg_keys[17], part), 18)
    return {
        "alignment": scatter_about(part_keys[0], (N_SEQ, N_RES, C_M), 1.0, 6.0, ((0, 32),)),
        "pair_rep": scatter_about(part_keys[1], (N_RES, N_RES, C_Z), 1.0, 6.0, ((0, 32),)),
        "align_mask": with_ends((jax.random.randint(part_keys[2], (N_SEQ, N_RES), 0, 8) < 7).astype(jnp.int32), jax.random.fold_in(part_keys[2], 1), 0, 1),
        "residue_mask": with_ends((jax.random.randint(part_keys[3], (N_RES,), 0, 16) < 15).astype(jnp.int32), jax.random.fold_in(part_keys[3], 1), 0, 1),
        "row_gain": jnp.clip(1.0 + 0.18 * jax.random.normal(arg_keys[4], (C_M,), jnp.float32), 0.1, 1.9),
        "pair_gain": jnp.clip(1.0 + 0.18 * jax.random.normal(arg_keys[5], (C_Z,), jnp.float32), 0.1, 1.9),
        "row_bias": scatter_about(arg_keys[6], (C_Z, HEADS), C_Z ** -0.5, 0.5),
        "row_scoring": draw_row_scoring(jax.random.fold_in(arg_keys[17], 71), part),
        "row_values": scatter_about(arg_keys[8], (C_M, 2 * C_M), C_M ** -0.5, 0.375),
        "row_output": scatter_about(arg_keys[9], (C_M, C_M), C_M ** -0.5, 0.375),
        "column_gain": jnp.clip(1.0 + 0.18 * jax.random.normal(arg_keys[10], (C_M,), jnp.float32), 0.1, 1.9),
        "column_scoring": draw_column_scoring(jax.random.fold_in(arg_keys[17], 71), part),
        "column_values": scatter_about(arg_keys[12], (C_M, 2 * C_M), C_M ** -0.5, 0.375),
        "column_output": scatter_about(arg_keys[13], (C_M, C_M), C_M ** -0.5, 0.375),
        "outer_gain": jnp.clip(1.0 + 0.18 * jax.random.normal(arg_keys[14], (C_M,), jnp.float32), 0.1, 1.9),
        "outer_inputs": scatter_about(arg_keys[15], (C_M, 2 * C_OPM), C_M ** -0.5, 0.375),
        "outer_output": scatter_about(arg_keys[16], (C_OPM * C_OPM, C_Z), C_OPM ** -0.5, 1.0),
    }


def layer_norm(values_in, gain):
    wide = values_in.astype(jnp.float32)
    average = lax.optimization_barrier(jnp.mean(wide, axis=-1, keepdims=True))
    centred = wide - average
    spread = lax.optimization_barrier(jnp.mean(centred * centred, axis=-1, keepdims=True))
    return (centred * lax.rsqrt(spread + 1e-05) * gain).astype(jnp.bfloat16)

def linear(inputs, weight):
    return jnp.einsum('...c,cd->...d', inputs.astype(jnp.float32), weight.astype(jnp.float32))

def attend_one(queries, keys_all, values_all, gates, keep_mask, bias_term):
    length_q = queries.shape[0]
    length_k = keys_all.shape[0]
    heads_q = queries.astype(jnp.float32).reshape(length_q, HEADS, HEAD)
    heads_k = keys_all.astype(jnp.float32).reshape(length_k, HEADS, HEAD)
    heads_v = values_all.astype(jnp.float32).reshape(length_k, HEADS, HEAD)
    scores = jnp.einsum('ihd,jhd->hij', heads_q, heads_k) / math.sqrt(HEAD) + bias_term
    scores = jnp.where(keep_mask[None, None, :] > 0, scores, -1000000000.0)
    weights = jax.nn.softmax(scores, axis=-1).astype(jnp.bfloat16)
    mixed = jnp.einsum('hij,jhd->ihd', weights.astype(jnp.float32), heads_v).reshape(length_q, HEADS * HEAD)
    return (mixed * jax.nn.sigmoid(gates.astype(jnp.float32))).astype(jnp.bfloat16)

def attention_layer(stream, gain, scoring, valuing, output, keep_mask, bias_term):
    normed = layer_norm(stream, gain)
    joint = linear(normed, scoring).astype(jnp.bfloat16)
    gated = linear(normed, valuing).astype(jnp.bfloat16)
    queries, keys_all = (joint[..., :C_M], joint[..., C_M:])
    values_all, gates = (gated[..., :C_M], gated[..., C_M:])

    def single(item):
        return attend_one(item[0], item[1], item[2], item[3], item[4], bias_term)
    mixed = lax.map(single, (queries, keys_all, values_all, gates, keep_mask))
    return (stream.astype(jnp.float32) + linear(mixed, output)).astype(jnp.bfloat16)

def reference(alignment, pair_rep, align_mask, residue_mask, row_gain, pair_gain, row_bias, row_scoring, row_values, row_output, column_gain, column_scoring, column_values, column_output, outer_gain, outer_inputs, outer_output):
    mask_float = align_mask.astype(jnp.float32)
    mask_narrow = align_mask.astype(jnp.bfloat16)
    residue_float = residue_mask.astype(jnp.float32)
    pair_bias = linear(layer_norm(pair_rep, pair_gain), row_bias).astype(jnp.bfloat16)
    bias_heads = jnp.transpose(pair_bias, (2, 0, 1)).astype(jnp.float32)
    keep_rows = mask_float * residue_float[None, :]
    first_update = attention_layer(alignment, row_gain, row_scoring, row_values, row_output, keep_rows, bias_heads)
    turned = jnp.swapaxes(first_update, 0, 1)
    second = attention_layer(turned, column_gain, column_scoring, column_values, column_output, jnp.swapaxes(mask_float, 0, 1), jnp.float32(0.0))
    new_alignment = jnp.swapaxes(second, 0, 1)
    outer_normed = layer_norm(new_alignment, outer_gain)
    sides = (linear(outer_normed, outer_inputs) * mask_float[..., None]).astype(jnp.bfloat16)
    left_side = sides[..., :C_OPM]
    right_side = sides[..., C_OPM:].astype(jnp.float32)
    pair_count = jnp.dot(jnp.swapaxes(mask_narrow, 0, 1), mask_narrow, preferred_element_type=jnp.float32)

    def one_row(item):
        left_row, count_row, pair_row, factor = item
        products = jnp.einsum('sc,sje->jce', left_row.astype(jnp.float32), right_side).astype(jnp.bfloat16)
        projected = jnp.dot(products.reshape(N_RES, C_OPM * C_OPM), outer_output, preferred_element_type=jnp.float32)
        scaled = projected / (0.001 + count_row)[:, None] * factor * residue_float[:, None]
        return (pair_row.astype(jnp.float32) + scaled).astype(jnp.bfloat16)
    new_pair = lax.map(one_row, (jnp.swapaxes(left_side, 0, 1), pair_count, pair_rep, residue_float))
    return (new_alignment, new_pair)
```

```python
import functools
import math

import jax
import jax.numpy as jnp
from jax import lax
from jax.experimental import pallas as pl
from jax.experimental.pallas import tpu as pltpu
from jax.sharding import PartitionSpec as P

HEADS = 8
HEAD = 32
C_OPM = 32
LOG2E = math.log2(math.e)
SCALE = LOG2E / math.sqrt(HEAD)
MASKED = -1000000000.0 * LOG2E
NT = (((1,), (1,)), ((), ()))
MESH = pl.DeviceIdType.MESH
VMEM = pl.BlockSpec(memory_space=pltpu.VMEM)
LIMIT = 48 * 1024 * 1024


def norm(wide, gain):
    average = jnp.mean(wide, axis=-1, keepdims=True)
    centred = wide - average
    spread = jnp.mean(centred * centred, axis=-1, keepdims=True)
    return (centred * lax.rsqrt(spread + 1e-05) * gain).astype(jnp.bfloat16)


def dot(a, b):
    return jnp.dot(a, b, preferred_element_type=jnp.float32)


def dot_nt(a, b):
    return lax.dot_general(a, b, NT, preferred_element_type=jnp.float32)


def greet(partners):
    barrier = pltpu.get_barrier_semaphore()
    for partner in partners:
        pl.semaphore_signal(barrier, inc=1, device_id={"dap": partner}, device_id_type=MESH)
    pl.semaphore_wait(barrier, len(partners))


def greet_all(n, me):
    barrier = pltpu.get_barrier_semaphore()

    def one(k, carry):
        pl.semaphore_signal(
            barrier, inc=1, device_id={"dap": lax.rem(me + k, n)}, device_id_type=MESH
        )
        return carry

    lax.fori_loop(1, n, one, 0)
    pl.semaphore_wait(barrier, n - 1)


class Gather:
    def __init__(self, n, me, out, zs, zr, ps, pr, cs, cr):
        self.n, self.me, self.out = n, me, out
        self.sems = {"z": (zs, zr), "p": (ps, pr), "c": (cs, cr)}
        self.layers = n // 8
        self.z = me // 8
        self.p = lax.rem(me // 2, 4)
        self.c = lax.rem(me, 2)

    def place(self, z, p, c):
        return z * 8 + p * 2 + c

    def plane(self, p, k):
        if k == 0:
            return p
        if k == 1:
            return p + 1 - 2 * lax.rem(p, 2)
        if k == 2:
            return lax.rem(p + 2, 4)
        return 3 - p

    def partners(self):
        found = [self.place(lax.rem(self.z + d, self.layers), self.p, self.c) for d in range(1, self.layers)]
        found += [self.place(self.z, self.plane(self.p, k), self.c) for k in (1, 2, 3)]
        return found + [self.place(self.z, self.p, 1 - self.c)]

    def copy(self, kind, slot, block, target):
        send, recv = self.sems[kind]
        return pltpu.make_async_remote_copy(
            src_ref=self.out.at[block],
            dst_ref=self.out.at[block],
            send_sem=send.at[slot],
            recv_sem=recv.at[slot],
            device_id={"dap": target},
            device_id_type=MESH,
        )

    def layer(self, d):
        return lax.rem(self.z + self.layers - d, self.layers)

    def z_copy(self, d):
        return self.copy("z", d, self.me, self.place(lax.rem(self.z + d, self.layers), self.p, self.c))

    def p_copy(self, d, k):
        block = self.place(self.layer(d), self.p, self.c)
        return self.copy("p", d * 4 + k, block, self.place(self.z, self.plane(self.p, k), self.c))

    def c_copy(self, d, k):
        block = self.place(self.layer(d), self.plane(self.p, k), self.c)
        return self.copy("c", d * 4 + k, block, self.place(self.z, self.p, 1 - self.c))

    def z_arrived(self, d):
        block = self.place(self.layer(d), self.p, self.c)
        self.copy("z", d, block, self.place(lax.rem(self.z + d, self.layers), self.p, self.c)).wait_recv()

    def p_arrived(self, d, k):
        block = self.place(self.layer(d), self.plane(self.p, k), self.c)
        self.copy("p", d * 4 + k, block, self.place(self.z, self.plane(self.p, k), self.c)).wait_recv()

    def c_arrived(self, d, k):
        block = self.place(self.layer(d), self.plane(self.p, k), 1 - self.c)
        self.copy("c", d * 4 + k, block, self.place(self.z, self.p, 1 - self.c)).wait_recv()

    def start(self):
        for d in range(1, self.layers):
            self.z_copy(d).start()
        for k in (1, 2, 3):
            self.p_copy(0, k).start()
        self.c_copy(0, 0).start()

    def relay(self):
        for d in range(1, self.layers):
            self.z_arrived(d)
            for k in (1, 2, 3):
                self.p_copy(d, k).start()
            self.c_copy(d, 0).start()
        for d in range(self.layers):
            for k in (1, 2, 3):
                self.p_arrived(d, k)
                self.c_copy(d, k).start()

    def finish(self):
        for d in range(self.layers):
            for k in range(4):
                self.c_arrived(d, k)
        for d in range(self.layers):
            if d > 0:
                self.z_copy(d).wait_send()
            for k in range(4):
                if k > 0:
                    self.p_copy(d, k).wait_send()
                self.c_copy(d, k).wait_send()


def gather_sems(n):
    layers = n // 8
    sizes = (layers, layers, layers * 4, layers * 4, layers * 4, layers * 4)
    return [pltpu.SemaphoreType.DMA((size,)) for size in sizes]


class Exchange:
    def __init__(self, n, me, src, dst, send, recv):
        self.n, self.me, self.src, self.dst, self.send, self.recv = n, me, src, dst, send, recv

    def copy(self, k, block_out, block_in):
        return pltpu.make_async_remote_copy(
            src_ref=self.src.at[block_out],
            dst_ref=self.dst.at[block_in],
            send_sem=self.send.at[k],
            recv_sem=self.recv.at[k],
            device_id={"dap": block_out},
            device_id_type=MESH,
        )

    def start(self):
        def one(k, carry):
            self.copy(k, lax.rem(self.me + k, self.n), self.me).start()
            return carry

        lax.fori_loop(1, self.n, one, 0)

    def finish(self):
        def one(k, carry):
            target = lax.rem(self.me + k, self.n)
            self.copy(k, target, lax.rem(self.me + self.n - k, self.n)).wait_recv()
            self.copy(k, target, self.me).wait_send()
            return carry

        lax.fori_loop(1, self.n, one, 0)


def bias_kernel(n, pair_ref, gain_ref, weight_ref, out_ref, turned, *sems):
    me = lax.axis_index("dap")
    gather = Gather(n, me, out_ref, *sems)
    rows = pair_ref.shape[0]
    for i in range(rows):
        normed = norm(pair_ref[i].astype(jnp.float32), gain_ref[...])
        turned[:, i, :] = dot_nt(weight_ref[...], normed)
    out_ref[me] = turned[...].reshape(out_ref.shape[1:]).astype(jnp.bfloat16)
    greet(gather.partners())
    gather.start()
    gather.relay()
    gather.finish()


def attend(joint, gated, keep, width, bias):
    queries, keys_all = joint[:, :width], joint[:, width:]
    values_all, gates = gated[:, :width], gated[:, width:]
    lanes = lax.broadcasted_iota(jnp.int32, (1, width), 1) // HEAD
    total = None
    for h in range(HEADS):
        mine = (lanes == h).astype(jnp.float32).astype(jnp.bfloat16)
        scores = dot_nt(queries * mine, keys_all) * SCALE
        if bias is not None:
            scores = scores + bias(h)
        scores = jnp.where(keep, scores, MASKED)
        powers = jnp.exp2(scores - jnp.max(scores, axis=-1, keepdims=True))
        weights = powers * (1.0 / jnp.sum(powers, axis=-1, keepdims=True))
        part = dot(weights.astype(jnp.bfloat16), values_all * mine)
        total = part if total is None else total + part
    return (total * jax.nn.sigmoid(gates.astype(jnp.float32))).astype(jnp.bfloat16)


def row_kernel(al_ref, bias_ref, keep_ref, gain_ref, scoring_ref, values_ref, output_ref, out_ref, wide):
    @pl.when(pl.program_id(0) == 0)
    def _():
        wide[...] = bias_ref[...].astype(jnp.float32) * LOG2E

    length, width = al_ref.shape[1:]
    stream = al_ref[0].astype(jnp.float32)
    normed = norm(stream, gain_ref[...])
    joint = dot(normed, scoring_ref[...]).astype(jnp.bfloat16)
    gated = dot(normed, values_ref[...]).astype(jnp.bfloat16)
    span = wide.shape[1] // HEADS

    def bias(h):
        return wide[:, h * span : (h + 1) * span, :].reshape(length, length)

    mixed = attend(joint, gated, keep_ref[0] > 0, width, bias)
    out_ref[0] = (stream + dot(mixed, output_ref[...])).astype(jnp.bfloat16)


def swap_kernel(n, src_ref, out_ref, send, recv):
    me = lax.axis_index("dap")
    exchange = Exchange(n, me, src_ref, out_ref, send, recv)
    greet_all(n, me)
    exchange.start()
    out_ref[me] = src_ref[me]
    exchange.finish()


def column_kernel(
    in_ref, keep_ref, gain_ref, scoring_ref, values_ref, output_ref, outer_gain_ref, sides_ref,
    new_ref, left_ref, right_ref, wide, turned,
):
    i = pl.program_id(0)
    rows, width = wide.shape[1:]

    @pl.when(i == 0)
    def _():
        wide[...] = in_ref[...].astype(jnp.float32).reshape(wide.shape)

    stream = wide[:, i, :]
    normed = norm(stream, gain_ref[...])
    joint = dot(normed, scoring_ref[...]).astype(jnp.bfloat16)
    gated = dot(normed, values_ref[...]).astype(jnp.bfloat16)
    keep = keep_ref[0]
    mixed = attend(joint, gated, keep > 0, width, None)
    second = (stream + dot(mixed, output_ref[...])).astype(jnp.bfloat16).astype(jnp.float32)
    wide[:, i, :] = second
    sides = dot_nt(sides_ref[...], norm(second, outer_gain_ref[...])) * keep
    left_ref[0] = sides[:C_OPM].astype(jnp.bfloat16)
    turned[:, i, :] = sides[C_OPM:]

    @pl.when(i == rows - 1)
    def _():
        new_ref[...] = wide[...].reshape(new_ref.shape).astype(jnp.bfloat16)
        right_ref[...] = turned[...].reshape(right_ref.shape).astype(jnp.bfloat16)


def spread_kernel(n, new_ref, right_ref, new_out, right_out, send, recv, *sems):
    me = lax.axis_index("dap")
    gather = Gather(n, me, right_out, *sems)
    exchange = Exchange(n, me, new_ref, new_out, send, recv)
    right_out[me] = right_ref[...]
    greet_all(n, me)
    gather.start()
    exchange.start()
    new_out[me] = new_ref[me]
    gather.relay()
    gather.finish()
    exchange.finish()


def outer_kernel(left_ref, right_ref, weight_ref, scale_ref, pair_ref, out_ref, wide, products):
    rows = pair_ref.shape[0]
    total = pair_ref.shape[1]
    span = wide.shape[1] // C_OPM
    left = left_ref[...].reshape(rows * C_OPM, left_ref.shape[2])
    wide[...] = right_ref[...].astype(jnp.float32)
    for e in range(C_OPM):
        piece = wide[:, e * span : (e + 1) * span, :].reshape(total, wide.shape[2])
        block = dot_nt(left, piece.astype(jnp.bfloat16)).astype(jnp.bfloat16)
        products[:, e * C_OPM : (e + 1) * C_OPM, :] = block.reshape(rows, C_OPM, total)
    for i in range(rows):
        flat = dot(weight_ref[...], products[i]) * scale_ref[i : i + 1, :]
        out_ref[i] = (pair_ref[i].astype(jnp.float32) + flat.T).astype(jnp.bfloat16)


def body(
    n,
    alignment,
    pair_rep,
    align_mask,
    residue_mask,
    row_gain,
    pair_gain,
    row_bias,
    row_scoring,
    row_values,
    row_output,
    column_gain,
    column_scoring,
    column_values,
    column_output,
    outer_gain,
    outer_inputs,
    outer_output,
):
    seqs, total_res, width = alignment.shape
    rows, _, channels = pair_rep.shape
    total_seqs = seqs * n
    narrow, wide = jnp.bfloat16, jnp.float32
    shape = jax.ShapeDtypeStruct
    me = lax.axis_index("dap")

    every_mask = lax.all_gather(align_mask, "dap", axis=0, tiled=True).astype(wide)
    residue_float = residue_mask.astype(wide)
    keep_rows = (align_mask.astype(wide) * residue_float[None, :])[:, None, :]
    keep_columns = lax.dynamic_slice_in_dim(every_mask, me * rows, rows, 1).T
    row_factor = lax.dynamic_slice_in_dim(residue_float, me * rows, rows)
    pair_count = jnp.dot(keep_columns, every_mask)
    scale = row_factor[:, None] * residue_float[None, :] / (0.001 + pair_count)
    turned_output = outer_output.reshape(C_OPM, C_OPM, channels).transpose(2, 1, 0).reshape(channels, -1)

    def params(**more):
        return pltpu.CompilerParams(vmem_limit_bytes=LIMIT, **more)

    every_bias = pl.pallas_call(
        functools.partial(bias_kernel, n),
        out_shape=shape((n, HEADS * rows, total_res), narrow),
        in_specs=[VMEM] * 3,
        out_specs=VMEM,
        scratch_shapes=[pltpu.VMEM((HEADS, rows, total_res), wide)] + gather_sems(n),
        compiler_params=params(collective_id=0, has_side_effects=True),
        name="bias_gather",
    )(pair_rep, pair_gain[None], row_bias.T)

    def whole(array):
        return pl.BlockSpec(array.shape, lambda i: (0,) * array.ndim)

    def one(*tail):
        return pl.BlockSpec((1,) + tail, lambda i: (i, 0, 0))

    first_update = pl.pallas_call(
        row_kernel,
        out_shape=shape(alignment.shape, narrow),
        grid=(seqs,),
        in_specs=[
            one(total_res, width), whole(every_bias), one(1, total_res), whole(row_gain[None]),
            whole(row_scoring), whole(row_values), whole(row_output),
        ],
        out_specs=one(total_res, width),
        scratch_shapes=[pltpu.VMEM(every_bias.shape, wide)],
        compiler_params=params(),
        name="row_attention",
    )(alignment, every_bias, keep_rows, row_gain[None], row_scoring, row_values, row_output)

    blocks = jnp.swapaxes(first_update.reshape(seqs, n, rows, width), 0, 1).reshape(n, seqs * rows, width)
    columns = pl.pallas_call(
        functools.partial(swap_kernel, n),
        out_shape=shape(blocks.shape, narrow),
        in_specs=[VMEM],
        out_specs=VMEM,
        scratch_shapes=[pltpu.SemaphoreType.DMA((n,)), pltpu.SemaphoreType.DMA((n,))],
        compiler_params=params(collective_id=1, has_side_effects=True),
        name="to_columns",
    )(blocks)

    turned_inputs = outer_inputs.T
    right_shape = (C_OPM * rows, total_seqs)
    new_blocks, left, right = pl.pallas_call(
        column_kernel,
        out_shape=(
            shape(blocks.shape, narrow),
            shape((rows, C_OPM, total_seqs), narrow),
            shape(right_shape, narrow),
        ),
        grid=(rows,),
        in_specs=[
            whole(columns), one(1, total_seqs), whole(column_gain[None]), whole(column_scoring),
            whole(column_values), whole(column_output), whole(outer_gain[None]), whole(turned_inputs),
        ],
        out_specs=(
            pl.BlockSpec(blocks.shape, lambda i: (0, 0, 0)),
            one(C_OPM, total_seqs),
            pl.BlockSpec(right_shape, lambda i: (0, 0)),
        ),
        scratch_shapes=[
            pltpu.VMEM((total_seqs, rows, width), wide),
            pltpu.VMEM((C_OPM, rows, total_seqs), wide),
        ],
        compiler_params=params(),
        name="column_attention",
    )(
        columns, keep_columns[:, None, :], column_gain[None], column_scoring, column_values,
        column_output, outer_gain[None], turned_inputs,
    )

    new_back, every_right = pl.pallas_call(
        functools.partial(spread_kernel, n),
        out_shape=(shape(blocks.shape, narrow), shape((n,) + right_shape, narrow)),
        in_specs=[VMEM] * 2,
        out_specs=(VMEM, VMEM),
        scratch_shapes=[pltpu.SemaphoreType.DMA((n,)), pltpu.SemaphoreType.DMA((n,))] + gather_sems(n),
        compiler_params=params(collective_id=2, has_side_effects=True),
        name="spread",
    )(new_blocks, right)

    new_pair = pl.pallas_call(
        outer_kernel,
        out_shape=shape(pair_rep.shape, narrow),
        in_specs=[VMEM] * 5,
        out_specs=VMEM,
        scratch_shapes=[
            pltpu.VMEM((n,) + right_shape, wide),
            pltpu.VMEM((rows, C_OPM * C_OPM, total_res), narrow),
        ],
        compiler_params=params(),
        name="outer_product",
    )(left, every_right, turned_output, scale, pair_rep)
    new_alignment = jnp.swapaxes(new_back.reshape(n, seqs, rows, width), 0, 1).reshape(alignment.shape)
    return new_alignment, new_pair


def solution(mesh):
    split = P(("dp", "dap"), None, None)
    in_specs = (split, split, P(("dp", "dap"), None), P("dp")) + (P(),) * 13
    return jax.shard_map(
        functools.partial(body, mesh.shape["dap"]),
        mesh=mesh,
        in_specs=in_specs,
        out_specs=(split, split),
        check_vma=False,
    )
```

```python
import functools
import math

import jax
import jax.numpy as jnp
from jax import lax
from jax.experimental import pallas as pl
from jax.experimental.pallas import tpu as pltpu
from jax.sharding import PartitionSpec as P

HEADS = 8
HEAD = 32
C_OPM = 32
LOG2E = math.log2(math.e)
SCALE = LOG2E / math.sqrt(HEAD)
MASKED = -1000000000.0 * LOG2E
NT = (((1,), (1,)), ((), ()))
MESH = pl.DeviceIdType.MESH
VMEM = pl.BlockSpec(memory_space=pltpu.VMEM)
LIMIT = 48 * 1024 * 1024


def norm(wide, gain):
    average = jnp.mean(wide, axis=-1, keepdims=True)
    centred = wide - average
    spread = jnp.mean(centred * centred, axis=-1, keepdims=True)
    return (centred * lax.rsqrt(spread + 1e-05) * gain).astype(jnp.bfloat16)


def dot(a, b):
    return jnp.dot(a, b, preferred_element_type=jnp.float32)


def dot_nt(a, b):
    return lax.dot_general(a, b, NT, preferred_element_type=jnp.float32)


def greet_all(n, me):
    barrier = pltpu.get_barrier_semaphore()

    def one(k, carry):
        pl.semaphore_signal(
            barrier, inc=1, device_id={"dap": lax.rem(me + k, n)}, device_id_type=MESH
        )
        return carry

    lax.fori_loop(1, n, one, 0)


def met_all(n):
    pl.semaphore_wait(pltpu.get_barrier_semaphore(), n - 1)


class Gather:
    def __init__(self, n, me, out, zs, zr, ps, pr, cs, cr):
        self.n, self.me, self.out = n, me, out
        self.sems = {"z": (zs, zr), "p": (ps, pr), "c": (cs, cr)}
        self.layers = n // 8
        self.z = me // 8
        self.p = lax.rem(me // 2, 4)
        self.c = lax.rem(me, 2)

    def place(self, z, p, c):
        return z * 8 + p * 2 + c

    def plane(self, p, k):
        if k == 0:
            return p
        if k == 1:
            return p + 1 - 2 * lax.rem(p, 2)
        if k == 2:
            return lax.rem(p + 2, 4)
        return 3 - p

    def copy(self, kind, slot, block, target):
        send, recv = self.sems[kind]
        return pltpu.make_async_remote_copy(
            src_ref=self.out.at[block],
            dst_ref=self.out.at[block],
            send_sem=send.at[slot],
            recv_sem=recv.at[slot],
            device_id={"dap": target},
            device_id_type=MESH,
        )

    def layer(self, d):
        return lax.rem(self.z + self.layers - d, self.layers)

    def z_copy(self, d):
        return self.copy("z", d, self.me, self.place(lax.rem(self.z + d, self.layers), self.p, self.c))

    def p_copy(self, d, k):
        block = self.place(self.layer(d), self.p, self.c)
        return self.copy("p", d * 4 + k, block, self.place(self.z, self.plane(self.p, k), self.c))

    def c_copy(self, d, k):
        block = self.place(self.layer(d), self.plane(self.p, k), self.c)
        return self.copy("c", d * 4 + k, block, self.place(self.z, self.p, 1 - self.c))

    def z_arrived(self, d):
        block = self.place(self.layer(d), self.p, self.c)
        self.copy("z", d, block, self.place(lax.rem(self.z + d, self.layers), self.p, self.c)).wait_recv()

    def p_arrived(self, d, k):
        block = self.place(self.layer(d), self.plane(self.p, k), self.c)
        self.copy("p", d * 4 + k, block, self.place(self.z, self.plane(self.p, k), self.c)).wait_recv()

    def c_arrived(self, d, k):
        block = self.place(self.layer(d), self.plane(self.p, k), 1 - self.c)
        self.copy("c", d * 4 + k, block, self.place(self.z, self.p, 1 - self.c)).wait_recv()

    def start(self):
        for d in range(1, self.layers):
            self.z_copy(d).start()
        for k in (1, 2, 3):
            self.p_copy(0, k).start()
        self.c_copy(0, 0).start()

    def relay_layers(self):
        for d in range(1, self.layers):
            self.z_arrived(d)
            for k in (1, 2, 3):
                self.p_copy(d, k).start()
            self.c_copy(d, 0).start()

    def relay_plane(self):
        for d in range(self.layers):
            for k in (1, 2, 3):
                self.p_arrived(d, k)
                self.c_copy(d, k).start()

    def finish(self):
        for d in range(self.layers):
            for k in range(4):
                self.c_arrived(d, k)
        for d in range(self.layers):
            if d > 0:
                self.z_copy(d).wait_send()
            for k in range(4):
                if k > 0:
                    self.p_copy(d, k).wait_send()
                self.c_copy(d, k).wait_send()


def gather_sems(n):
    layers = n // 8
    sizes = (layers, layers, layers * 4, layers * 4, layers * 4, layers * 4)
    return [pltpu.SemaphoreType.DMA((size,)) for size in sizes]


class Exchange:
    def __init__(self, n, me, src, dst, piece, send, recv):
        self.n, self.me, self.src, self.dst = n, me, src, dst
        self.rows, self.first = pl.ds(piece * 16, 16), piece * n
        self.send, self.recv = send, recv

    def copy(self, k, block_out, block_in):
        return pltpu.make_async_remote_copy(
            src_ref=self.src.at[block_out, self.rows],
            dst_ref=self.dst.at[block_in, self.rows],
            send_sem=self.send.at[self.first + k],
            recv_sem=self.recv.at[self.first + k],
            device_id={"dap": block_out},
            device_id_type=MESH,
        )

    def start(self):
        def one(k, carry):
            self.copy(k, lax.rem(self.me + k, self.n), self.me).start()
            return carry

        lax.fori_loop(1, self.n, one, 0)
        self.dst[self.me, self.rows] = self.src[self.me, self.rows]

    def finish(self):
        def one(k, carry):
            target = lax.rem(self.me + k, self.n)
            self.copy(k, target, lax.rem(self.me + self.n - k, self.n)).wait_recv()
            self.copy(k, target, self.me).wait_send()
            return carry

        lax.fori_loop(1, self.n, one, 0)


def attend(joint, gated, keeps, width, bias):
    queries, keys_all = joint[:, :width], joint[:, width:]
    values_all, gates = gated[:, :width], gated[:, width:]
    groups = len(keeps)
    length = joint.shape[0] // groups
    lanes = lax.broadcasted_iota(jnp.int32, (1, width), 1) // HEAD
    totals = [None] * groups
    for h in range(HEADS):
        mine = (lanes == h).astype(jnp.float32).astype(jnp.bfloat16)
        asked, given = queries * mine, values_all * mine
        for g in range(groups):
            part = slice(g * length, (g + 1) * length)
            scores = dot_nt(asked[part], keys_all[part]) * SCALE
            if bias is not None:
                scores = scores + bias(h)
            scores = jnp.where(keeps[g], scores, MASKED)
            powers = jnp.exp2(scores - jnp.max(scores, axis=-1, keepdims=True))
            weights = powers * (1.0 / jnp.sum(powers, axis=-1, keepdims=True))
            mixed = dot(weights.astype(jnp.bfloat16), given[part])
            totals[g] = mixed if totals[g] is None else totals[g] + mixed
    total = jnp.concatenate(totals, axis=0) if groups > 1 else totals[0]
    return (total * jax.nn.sigmoid(gates.astype(jnp.float32))).astype(jnp.bfloat16)


N_IN = 17


def kernel(n, *refs):
    inputs, (back, new_pair), scratch = refs[:N_IN], refs[N_IN : N_IN + 2], refs[N_IN + 2 :]
    held, scratch = scratch[:N_IN], scratch[N_IN:]
    (
        turned, every_bias, wide_bias, joints, gates, stage, sent, columns, wide, turned_right,
        new_sent, left, every_right, wide_right, products, wide_output, turned_output, in_sems,
        ex_send, ex_recv, back_send, back_recv, *sems,
    ) = scratch
    (
        alignment, pair_rep, align_mask, residue_mask, row_gain, pair_gain, row_bias, row_scoring,
        row_values, row_output, column_gain, column_scoring, column_values, column_output,
        outer_gain, outer_inputs, outer_output,
    ) = held
    narrow, full = jnp.bfloat16, jnp.float32
    me = lax.axis_index("dap")
    seqs, total_res, width = alignment.shape
    rows = pair_rep.shape[0]
    total_seqs = seqs * n
    half = rows // 2

    order = (1, 5, 6, 2, 0, 4, 7, 8, 3, 9, 10, 11, 12, 13, 14, 15, 16)
    loads = [pltpu.make_async_copy(inputs[k], held[k], in_sems.at[k]) for k in range(N_IN)]
    for k in order:
        loads[k].start()
    greet_all(n, me)

    for k in (1, 5, 6, 2):
        loads[k].wait()
    for i in range(rows):
        normed = norm(pair_rep[i].astype(full), pair_gain[...])
        turned[:HEADS, i, :] = dot_nt(row_bias[...], normed)
    turned[HEADS] = jnp.zeros(turned.shape[1:], full)
    turned[HEADS + 1] = jnp.zeros(turned.shape[1:], full)
    turned[HEADS, :seqs, :] = align_mask[...].astype(full)
    every_bias[me] = turned[...].reshape(every_bias.shape[1:]).astype(narrow)
    met_all(n)
    gather = Gather(n, me, every_bias, *sems[:6])
    gather.start()

    def project(s, carry):
        normed = norm(alignment[s].astype(full), row_gain[...])
        joints[s] = dot(normed, row_scoring[...]).astype(narrow)
        gates[s] = dot(normed, row_values[...]).astype(narrow)
        return carry

    for k in (0, 4, 7, 8):
        loads[k].wait()
    lax.fori_loop(0, seqs // 2, project, 0)
    gather.relay_layers()
    lax.fori_loop(seqs // 2, seqs, project, 0)
    gather.relay_plane()
    for k in (3, 9, 10, 11, 12, 13, 14, 15, 16):
        loads[k].wait()
    wide_output[...] = outer_output[...].astype(full).reshape(wide_output.shape)
    for g in range(C_OPM // 4):
        piece = jnp.concatenate([wide_output[:, g * 4 + t, :] for t in range(4)], axis=0)
        turned_output[:, g * 128 : (g + 1) * 128] = piece.T.astype(narrow)
    gather.finish()

    wide_bias[...] = every_bias[:, : HEADS * rows, :].astype(full) * LOG2E
    every_mask = every_bias[:, HEADS * rows :, :].astype(full)[:, :rows, :].reshape(n * rows, total_res)
    place = lax.broadcasted_iota(jnp.int32, (total_seqs, n * rows), 0)
    spot = lax.broadcasted_iota(jnp.int32, (total_seqs, n * rows), 1)
    pick = (spot == place // seqs * rows + place % seqs).astype(full).astype(narrow)
    mask = dot(pick, every_mask.astype(narrow)).astype(narrow)
    near = lax.broadcasted_iota(jnp.int32, (rows, total_res), 1) - me * rows
    own = (near == lax.broadcasted_iota(jnp.int32, (rows, total_res), 0)).astype(full)
    keep_columns = dot_nt(own.astype(narrow), mask)
    residue_float = residue_mask[...].astype(full)
    row_factor = jnp.sum(own * residue_float, axis=-1, keepdims=True)
    pair_count = dot(keep_columns.astype(narrow), mask)
    scale = row_factor * residue_float / (0.001 + pair_count)

    def bias(h):
        return wide_bias[:, h * rows : (h + 1) * rows, :].reshape(total_res, total_res)

    to_columns = []
    for piece in range(2):
        for t in range(2):
            s = piece * 2 + t
            keep = align_mask[s : s + 1, :].astype(full) * residue_float
            mixed = attend(joints[s], gates[s], [keep > 0], width, bias)
            updated = alignment[s].astype(full) + dot(mixed, row_output[...])
            stage[:, t] = updated.reshape(n, rows, width)
        sent[:, piece * 16 : (piece + 1) * 16, :] = stage[...].reshape(n, 16, width).astype(narrow)
        to_columns.append(Exchange(n, me, sent, columns, piece, ex_send, ex_recv))
        to_columns[piece].start()
    for piece in range(2):
        to_columns[piece].finish()

    wide[...] = columns[...].astype(full).reshape(wide.shape)
    backwards = []
    for piece in range(2):
        mine = range(piece * half, (piece + 1) * half)
        stream = jnp.concatenate([wide[:, i, :] for i in mine], axis=0)
        normed = norm(stream, column_gain[...])
        joint = dot(normed, column_scoring[...]).astype(narrow)
        gated = dot(normed, column_values[...]).astype(narrow)
        keeps = [keep_columns[i : i + 1, :] > 0 for i in mine]
        mixed = attend(joint, gated, keeps, width, None)
        second = (stream + dot(mixed, column_output[...])).astype(narrow).astype(full)
        outer_normed = norm(second, outer_gain[...])
        for t, i in enumerate(mine):
            part = slice(t * total_seqs, (t + 1) * total_seqs)
            sides = dot_nt(outer_inputs[...], outer_normed[part]) * keep_columns[i : i + 1, :]
            left[i] = sides[:C_OPM].astype(narrow)
            turned_right[:, i, :] = sides[C_OPM:]
            wide[:, i, :] = second[part]
        block = wide[:, piece * half : (piece + 1) * half, :].reshape(n, 16, width)
        new_sent[:, piece * 16 : (piece + 1) * 16, :] = block.astype(narrow)
        backwards.append(Exchange(n, me, new_sent, back, piece, back_send, back_recv))
        if piece == 0:
            backwards[0].start()
    every_right[me] = turned_right[...].reshape(every_right.shape[1:]).astype(narrow)
    gather = Gather(n, me, every_right, *sems[6:])
    gather.start()
    gather.relay_layers()
    gather.relay_plane()
    backwards[1].start()
    gather.finish()

    sides = left[...].reshape(rows * C_OPM, total_seqs)
    wide_right[...] = every_right[...].astype(full)
    for e in range(C_OPM):
        piece = wide_right[:, e * rows : (e + 1) * rows, :].reshape(total_res, total_seqs)
        block = dot_nt(sides, piece.astype(narrow)).astype(narrow)
        products[:, e * C_OPM : (e + 1) * C_OPM, :] = block.reshape(rows, C_OPM, total_res)
    for i in range(rows):
        flat = dot(turned_output[...], products[i]) * scale[i : i + 1, :]
        new_pair[i] = (pair_rep[i].astype(full) + flat.T).astype(narrow)
    for piece in range(2):
        backwards[piece].finish()


def body(n, alignment, pair_rep, align_mask, residue_mask, *rest):
    (
        row_gain, pair_gain, row_bias, row_scoring, row_values, row_output, column_gain,
        column_scoring, column_values, column_output, outer_gain, outer_inputs, outer_output,
    ) = rest
    seqs, total_res, width = alignment.shape
    rows, _, channels = pair_rep.shape
    total_seqs = seqs * n
    narrow, full = jnp.bfloat16, jnp.float32
    arguments = (
        alignment, pair_rep, align_mask, residue_mask[None], row_gain[None], pair_gain[None],
        row_bias.T, row_scoring, row_values, row_output, column_gain[None], column_scoring,
        column_values, column_output, outer_gain[None], outer_inputs.T, outer_output,
    )
    dma = pltpu.SemaphoreType.DMA
    blocks = (n, seqs * rows, width)
    right_shape = (C_OPM * rows, total_seqs)
    flat = C_OPM * C_OPM
    back, new_pair = pl.pallas_call(
        functools.partial(kernel, n),
        out_shape=(
            jax.ShapeDtypeStruct(blocks, narrow),
            jax.ShapeDtypeStruct(pair_rep.shape, narrow),
        ),
        in_specs=[pl.BlockSpec(memory_space=pl.ANY)] * N_IN,
        out_specs=(VMEM, VMEM),
        scratch_shapes=[pltpu.VMEM(array.shape, array.dtype) for array in arguments]
        + [
            pltpu.VMEM((HEADS + 2, rows, total_res), full),
            pltpu.VMEM((n, (HEADS + 2) * rows, total_res), narrow),
            pltpu.VMEM((n, HEADS * rows, total_res), full),
            pltpu.VMEM((seqs, total_res, 2 * width), narrow),
            pltpu.VMEM((seqs, total_res, 2 * width), narrow),
            pltpu.VMEM((n, 2, rows, width), full),
            pltpu.VMEM(blocks, narrow),
            pltpu.VMEM(blocks, narrow),
            pltpu.VMEM((total_seqs, rows, width), full),
            pltpu.VMEM((C_OPM, rows, total_seqs), full),
            pltpu.VMEM(blocks, narrow),
            pltpu.VMEM((rows, C_OPM, total_seqs), narrow),
            pltpu.VMEM((n,) + right_shape, narrow),
            pltpu.VMEM((n,) + right_shape, full),
            pltpu.VMEM((rows, flat, total_res), narrow),
            pltpu.VMEM((C_OPM, C_OPM, channels), full),
            pltpu.VMEM((channels, flat), narrow),
            dma((N_IN,)),
        ]
        + [dma((2 * n,))] * 4
        + gather_sems(n)
        + gather_sems(n),
        compiler_params=pltpu.CompilerParams(
            vmem_limit_bytes=LIMIT, collective_id=0, has_side_effects=True
        ),
        name="evoformer",
    )(*arguments)
    back = back.reshape(n, 2, seqs, rows // 2, width).transpose(2, 0, 1, 3, 4)
    return back.reshape(alignment.shape), new_pair


def solution(mesh):
    split = P(("dp", "dap"), None, None)
    in_specs = (split, split, P(("dp", "dap"), None), P("dp")) + (P(),) * 13
    return jax.shard_map(
        functools.partial(body, mesh.shape["dap"]),
        mesh=mesh,
        in_specs=in_specs,
        out_specs=(split, split),
        check_vma=False,
    )
```
